32 devices in a mesh: shard: 8 (over z, x), tensor: 4 (over y, core).
Axes of the slice: x: 2, y: 2, z: 4, core: 2. Of those that a mesh axis runs over, the one named last changes fastest.
Arguments:
- grads: bfloat16 [8, 4, 1536, 1024], P('shard', None, None, 'tensor'), may hold values from -240 to 240
- master: float32 [1536, 1024], P('shard', 'tensor'), may hold values from -3 to 3
- moment1: float32 [1536, 1024], P('shard', 'tensor'), may hold values from -3 to 3
- moment2: float32 [1536, 1024], P('shard', 'tensor'), may hold values from 0.25 to 1
- ema: float32 [1536, 1024], P('shard', 'tensor'), may hold values from -3 to 3
Outputs:
- new_master: float32 [1536, 1024], P('shard', 'tensor')
- new_moment1: float32 [1536, 1024], P('shard', 'tensor')
- new_moment2: float32 [1536, 1024], P('shard', 'tensor')
- new_ema: float32 [1536, 1024], P('shard', 'tensor')
- weights: bfloat16 [1536, 1024], P(None, 'tensor')
The draws below stay inside these ranges and needn't reach their ends.
All inputs are finite; a program needn't handle non-finite values.
Results may differ from the reference program's by a relative error of at most 0.0004.
Values may be sent and summed in bfloat16 or wider, within the bound.
A program may use at most 64 MiB of HBM per device.

```python
import math
import jax
import jax.numpy as jnp
from jax import lax

D = 1536
MICRO = 4
STEP = 10
COLS = 1024
ELEMS = 1572864
N_SHARD = 8


def draw_grads(key, part):
    keys = jax.random.split(key, 3)
    shape = (N_SHARD, MICRO, D, COLS)
    rows = jnp.arange(D, dtype=jnp.float32) / D
    base = jnp.clip(jax.random.normal(keys[0], shape, jnp.float32), -6.0, 6.0)
    row_scale = 10.0 ** rows
    col_scale = jnp.exp(jax.random.uniform(keys[1], (COLS,), jnp.float32) * jnp.log(10.0))
    paired = jax.random.permutation(keys[2], N_SHARD)
    block = jnp.arange(D) // (D // N_SHARD)
    spike = jnp.where(block[None, :] == paired[:, None], 4.0, 1.0)
    values = 0.1 * base * row_scale[None, None, :, None] * col_scale[None, None, None, :] * spike[:, None, :, None]
    return values.astype(jnp.bfloat16)


def block_levels(stream_key, extent, cuts, low, high):
    loudness = 1.0
    for dim, shards_of in cuts:
        heights = jax.random.uniform(jax.random.fold_in(jax.random.fold_in(stream_key, 6), dim), (shards_of,), jnp.float32, low / len(cuts), high / len(cuts))
        loudness = loudness * jnp.repeat(jnp.exp(heights), extent[dim] // shards_of).reshape((-1,) + (1,) * (len(extent) - 1 - dim))
    return loudness


def gaussian(key, dims, width, most, cuts=(), kind=jnp.bfloat16):
    entries = jax.random.normal(key, dims, jnp.float32) * width
    if len(cuts) > 0:
        entries = block_levels(key, dims, cuts, -0.22, 0.18) * entries
    return jnp.clip(entries, min=-most, max=most).astype(kind)


def setup_inputs(seed: int = 0) -> dict:
    seeds = jax.random.split(jax.random.key(seed), 6)
    return {
        "grads": draw_grads(jax.random.fold_in(seeds[5], 71), 0),
        "master": gaussian(seeds[1], (D, COLS), 0.5, 3.0, ((0, 8), (1, 4)), jnp.float32),
        "moment1": gaussian(seeds[2], (D, COLS), 0.5, 3.0, ((0, 8), (1, 4)), jnp.float32),
        "moment2": jnp.clip(jnp.exp(math.log(1.0) - 1.3862944 * jax.random.uniform(seeds[3], (D, COLS), jnp.float32) ** block_levels(seeds[3], (D, COLS), ((0, 8), (1, 4)), -0.2, 0.2)), 0.25, 1.0),
        "ema": gaussian(seeds[4], (D, COLS), 0.5, 3.0, ((0, 8), (1, 4)), jnp.float32),
    }


def reference(grads, master, moment1, moment2, ema):

    def add_replica(carry, piece):
        return (carry + lax.optimization_barrier(jnp.sum(piece.astype(jnp.float32), axis=0)), None)
    total, unused = lax.scan(add_replica, jnp.zeros((D, COLS), jnp.float32), grads)
    sq = jnp.sum(total * total)
    scale = jnp.minimum(1.0, 1.0 / jnp.sqrt(sq / ELEMS + 1e-06))
    clipped = scale * total
    new_moment1 = 0.9 * moment1 + 0.1 * clipped
    new_moment2 = 0.95 * moment2 + 0.05 * clipped * clipped
    first_hat = new_moment1 / (1.0 - 0.9 ** STEP)
    second_hat = new_moment2 / (1.0 - 0.95 ** STEP)
    new_master = master - 0.02 * (first_hat / (jnp.sqrt(second_hat) + 1e-08) + 0.1 * master)
    new_ema = 0.99 * ema + 0.01 * new_master
    weights = new_master.astype(jnp.bfloat16)
    return (new_master, new_moment1, new_moment2, new_ema, weights)
```

```python
import jax
import jax.numpy as jnp
from jax import lax
from jax.experimental import pallas as pl
from jax.experimental.pallas import tpu as pltpu
from jax.sharding import PartitionSpec as P

STEP = 10

beta_one = 0.9
beta_two = 0.95
learn_rate = 0.02
decay_weight = 0.1
ema_keep = 0.99

MESH = pl.DeviceIdType.MESH
TILE = 32

GAIN = 16.0
LINEAR = 2.0**-12


def encode(value):
    u = jnp.abs(value) * GAIN
    u2 = u * u
    u4 = u2 * u2
    power = jnp.where(u < LINEAR, u * LINEAR**7, u4 * u4)
    return jnp.where(value < 0, -power, power).astype(jnp.bfloat16)


def decode(code):
    y = code.astype(jnp.float32)
    a = jnp.abs(y)
    fourth = lax.rsqrt(lax.rsqrt(a))
    root = jnp.where(a < LINEAR**8, a * (LINEAR**-7 / GAIN), fourth * lax.rsqrt(fourth) * (1.0 / GAIN))
    return jnp.where(y < 0, -root, root)


def plain(grads, master, moment1, moment2, ema):
    local = grads[0]
    elements = local.shape[1] * local.shape[2] * lax.axis_size("tensor")
    summed = jnp.sum(local.astype(jnp.float32), axis=0)
    grad_part = lax.psum_scatter(summed, "shard", scatter_dimension=0, tiled=True)
    sq = lax.psum(jnp.sum(grad_part * grad_part), ("shard", "tensor"))
    scale = jnp.minimum(1.0, 1.0 / jnp.sqrt(sq / elements + 1e-06))
    clipped = scale * grad_part
    new_moment1 = beta_one * moment1 + (1.0 - beta_one) * clipped
    new_moment2 = beta_two * moment2 + (1.0 - beta_two) * clipped * clipped
    first_hat = new_moment1 / (1.0 - beta_one**STEP)
    second_hat = new_moment2 / (1.0 - beta_two**STEP)
    new_master = master - learn_rate * (
        first_hat / (jnp.sqrt(second_hat) + 1e-08) + decay_weight * master
    )
    new_ema = ema_keep * ema + (1.0 - ema_keep) * new_master
    weights = lax.all_gather(new_master.astype(jnp.bfloat16), "shard", axis=0, tiled=True)
    return (new_master, new_moment1, new_moment2, new_ema, weights)


def make_kernel(n_tensor, micro, rows, cols):
    n_shard = 8
    elements = n_shard * rows * cols * n_tensor

    def kernel(g, ma, m1, m2, em, o_ma, o_m1, o_m2, o_em, o_w,
               gv, st, out, part, sx, rx, sz, rz, w, sq_a, sq_b,
               load_sem, store_sem, send_sem, recv_sem, sqs_sem, sqr_sem):
        s = lax.axis_index("shard")
        t = lax.axis_index("tensor")
        x = lax.rem(s, 2)
        z = s // 2
        other = 1 - x
        zs = (z, z + 1 - 2 * lax.rem(z, 2), lax.rem(z + 2, 4), 3 - z)
        to_x = {"shard": 2 * z + other}
        to_z = {1: {"shard": 2 * zs[1] + x}, 2: {"shard": 2 * zs[2] + x}}
        order = (3, 2, 1, 0)

        def block(j, xx):
            return pl.ds(pl.multiple_of((2 * zs[j] + xx) * rows, rows), rows)

        loads = {}
        for i, (j, mine) in enumerate([(j, False) for j in order] + [(j, True) for j in order]):
            loads[j, mine] = (i, pltpu.make_async_copy(
                g.at[0, :, block(j, x if mine else other), :], gv.at[i], load_sem.at[i]))
            loads[j, mine][1].start()
        state = []
        for i, ref in enumerate((ma, m1, m2, em)):
            state.append(pltpu.make_async_copy(ref, st.at[i], load_sem.at[8 + i]))
            state[-1].start()

        barrier = pltpu.get_barrier_semaphore()
        for k in range(1, n_shard):
            pl.semaphore_signal(barrier, inc=1, device_id={"shard": lax.rem(s + k, n_shard)}, device_id_type=MESH)
        for k in range(1, n_tensor):
            pl.semaphore_signal(barrier, inc=1, device_id={"tensor": lax.rem(t + k, n_tensor)}, device_id_type=MESH)

        def tiles(body, init=0):
            def step(i, carry):
                return body(pl.ds(pl.multiple_of(i * TILE, TILE), TILE), carry)
            return lax.fori_loop(0, rows // TILE, step, init)

        def micro_sum(slot, r):
            total = gv[slot, 0, r, :].astype(jnp.float32)
            for m in range(1, micro):
                total = total + gv[slot, m, r, :].astype(jnp.float32)
            return total

        sent = []

        def send(src, dst, index, target):
            copy = pltpu.make_async_remote_copy(
                src_ref=src, dst_ref=dst, send_sem=send_sem.at[index], recv_sem=recv_sem.at[index],
                device_id=target, device_id_type=MESH)
            copy.start()
            sent.append(copy)
            return copy

        over_x = {}
        for n, j in enumerate(order):
            slot, copy = loads[j, False]
            copy.wait()

            def body(r, c, slot=slot, j=j):
                sx[j, r, :] = encode(micro_sum(slot, r))
                return c
            tiles(body)
            if n == 0:
                pl.semaphore_wait(barrier, n_shard - 1 + n_tensor - 1)
            over_x[j] = send(sx.at[j], rx.at[j], j, to_x)

        for j in order:
            slot, copy = loads[j, True]
            copy.wait()

            def body(r, c, slot=slot, j=j):
                part[j, r, :] = micro_sum(slot, r)
                return c
            tiles(body)

        over_x[3].wait_recv()

        def body(r, c):
            sz[0, r, :] = encode(part[3, r, :] + decode(rx[3, r, :]))
            return c
        tiles(body)
        first = send(sz.at[0], rz.at[0], 4, to_z[1])

        over_x[2].wait_recv()
        first.wait_recv()

        def body(r, c):
            sz[1, r, :] = encode(part[2, r, :] + decode(rx[2, r, :]) + decode(rz[0, r, :]))
            return c
        tiles(body)
        far = send(sz.at[1], rz.at[1], 5, to_z[2])

        over_x[1].wait_recv()

        def body(r, c):
            sz[2, r, :] = encode(part[1, r, :] + decode(rx[1, r, :]))
            return c
        tiles(body)
        near = send(sz.at[2], rz.at[2], 6, to_z[1])

        over_x[0].wait_recv()

        def body(r, c):
            part[0, r, :] = part[0, r, :] + decode(rx[0, r, :])
            return c
        tiles(body)
        near.wait_recv()

        def body(r, c):
            part[0, r, :] = part[0, r, :] + decode(rz[2, r, :])
            return c
        tiles(body)
        far.wait_recv()

        def body(r, acc):
            total = part[0, r, :] + decode(rz[1, r, :])
            part[0, r, :] = total
            square = total * total
            square = square[:, :cols // 2] + square[:, cols // 2:]
            return acc + jnp.sum(square.reshape(TILE // 8, 8, cols // 2), axis=0)
        acc = tiles(body, jnp.zeros((8, cols // 2), jnp.float32))

        def gather(buffer, axis, me, count, base):
            copies = []
            for k in range(1, count):
                copies.append(pltpu.make_async_remote_copy(
                    src_ref=buffer.at[me], dst_ref=buffer.at[me],
                    send_sem=sqs_sem.at[base + k], recv_sem=sqr_sem.at[base + k],
                    device_id={axis: lax.rem(me + k, count)}, device_id_type=MESH))
                copies[-1].start()
            for copy in copies:
                copy.wait_recv()
            sent.extend(copies)
            total = buffer[0]
            for i in range(1, count):
                total = total + buffer[i]
            return total

        sq_a[s] = jnp.sum(acc, axis=0, keepdims=True)
        sq_b[t] = gather(sq_a, "shard", s, n_shard, 0)
        sq = jnp.sum(gather(sq_b, "tensor", t, n_tensor, n_shard), axis=1, keepdims=True)
        scale = jnp.minimum(1.0, 1.0 / jnp.sqrt(sq / elements + 1e-06))

        for copy in state:
            copy.wait()

        def body(r, c):
            clipped = scale * part[0, r, :]
            new_m1 = beta_one * st[1, r, :] + (1.0 - beta_one) * clipped
            new_m2 = beta_two * st[2, r, :] + (1.0 - beta_two) * clipped * clipped
            first_hat = new_m1 / (1.0 - beta_one**STEP)
            second_hat = new_m2 / (1.0 - beta_two**STEP)
            old = st[0, r, :]
            new_ma = old - learn_rate * (first_hat / (jnp.sqrt(second_hat) + 1e-08) + decay_weight * old)
            w[s, r, :] = new_ma.astype(jnp.bfloat16)
            out[0, r, :] = new_ma
            out[1, r, :] = new_m1
            out[2, r, :] = new_m2
            return c
        tiles(body)

        def gathered(slot, index, target):
            return send(w.at[slot], w.at[slot], index, target)

        slot_x = [2 * zj + x for zj in zs]
        slot_o = [2 * zj + other for zj in zs]
        far = gathered(s, 9, to_z[2])
        near = gathered(s, 8, to_z[1])
        side = gathered(s, 7, to_x)

        stores = []

        def store(src, dst):
            copy = pltpu.make_async_copy(src, dst, store_sem.at[len(stores)])
            copy.start()
            stores.append(copy)

        def store_w(slot):
            store(w.at[slot], o_w.at[pl.ds(pl.multiple_of(slot * rows, rows), rows), :])

        store(out.at[0], o_ma)
        store(out.at[1], o_m1)
        store(out.at[2], o_m2)
        store_w(s)

        def body(r, c):
            out[3, r, :] = ema_keep * st[3, r, :] + (1.0 - ema_keep) * out[0, r, :]
            return c
        tiles(body)
        store(out.at[3], o_em)

        near.wait_recv()
        side_1 = gathered(slot_x[1], 11, to_x)
        store_w(slot_x[1])
        far.wait_recv()
        near_2 = gathered(slot_x[2], 10, to_z[1])
        side_2 = gathered(slot_x[2], 12, to_x)
        store_w(slot_x[2])
        side.wait_recv()
        store_w(slot_o[0])
        near_2.wait_recv()
        side_3 = gathered(slot_x[3], 13, to_x)
        store_w(slot_x[3])
        for copy, j in ((side_1, 1), (side_2, 2), (side_3, 3)):
            copy.wait_recv()
            store_w(slot_o[j])
        for copy in sent:
            copy.wait_send()
        for copy in stores:
            copy.wait()

    return kernel


def fused(grads, master, moment1, moment2, ema):
    n_tensor = lax.axis_size("tensor")
    micro = grads.shape[1]
    rows, cols = master.shape
    f32 = jax.ShapeDtypeStruct((rows, cols), jnp.float32)
    full = jax.ShapeDtypeStruct((8 * rows, cols), jnp.bfloat16)
    hbm = pl.BlockSpec(memory_space=pl.ANY)
    return pl.pallas_call(
        make_kernel(n_tensor, micro, rows, cols),
        out_shape=(f32, f32, f32, f32, full),
        in_specs=[hbm] * 5,
        out_specs=(hbm,) * 5,
        scratch_shapes=[
            pltpu.VMEM((8, micro, rows, cols), jnp.bfloat16),
            pltpu.VMEM((4, rows, cols), jnp.float32),
            pltpu.VMEM((4, rows, cols), jnp.float32),
            pltpu.VMEM((4, rows, cols), jnp.float32),
            pltpu.VMEM((4, rows, cols), jnp.bfloat16),
            pltpu.VMEM((4, rows, cols), jnp.bfloat16),
            pltpu.VMEM((3, rows, cols), jnp.bfloat16),
            pltpu.VMEM((3, rows, cols), jnp.bfloat16),
            pltpu.VMEM((8, rows, cols), jnp.bfloat16),
            pltpu.VMEM((8, 1, cols // 2), jnp.float32),
            pltpu.VMEM((n_tensor, 1, cols // 2), jnp.float32),
            pltpu.SemaphoreType.DMA((12,)),
            pltpu.SemaphoreType.DMA((12,)),
            pltpu.SemaphoreType.DMA((14,)),
            pltpu.SemaphoreType.DMA((14,)),
            pltpu.SemaphoreType.DMA((8 + n_tensor,)),
            pltpu.SemaphoreType.DMA((8 + n_tensor,)),
        ],
        compiler_params=pltpu.CompilerParams(
            collective_id=0, has_side_effects=True, vmem_limit_bytes=32 * 1024 * 1024
        ),
        cost_estimate=pl.CostEstimate(flops=20_000_000, bytes_accessed=6_000_000, transcendentals=300_000),
    )(grads, master, moment1, moment2, ema)


def solution(mesh):
    def shards(grads, master, moment1, moment2, ema):
        if mesh.shape["shard"] == 8 and master.shape[0] % TILE == 0 and master.shape[1] == 256:
            return fused(grads, master, moment1, moment2, ema)
        return plain(grads, master, moment1, moment2, ema)

    return jax.shard_map(
        shards,
        mesh=mesh,
        in_specs=(
            P("shard", None, None, "tensor"),
            P("shard", "tensor"),
            P("shard", "tensor"),
            P("shard", "tensor"),
            P("shard", "tensor"),
        ),
        out_specs=(
            P("shard", "tensor"),
            P("shard", "tensor"),
            P("shard", "tensor"),
            P("shard", "tensor"),
            P(None, "tensor"),
        ),
        check_vma=False,
    )
```

```python
import jax
import jax.numpy as jnp
from jax import lax
from jax.experimental import pallas as pl
from jax.experimental.pallas import tpu as pltpu
from jax.sharding import PartitionSpec as P

STEP = 10

beta_one = 0.9
beta_two = 0.95
learn_rate = 0.02
decay_weight = 0.1
ema_keep = 0.99

MESH = pl.DeviceIdType.MESH
TILE = 32
PIECES = 2

GAIN = 16.0
LINEAR = 2.0**-12


def encode(value):
    u = jnp.abs(value) * GAIN
    u2 = u * u
    u4 = u2 * u2
    power = jnp.where(u < LINEAR, u * LINEAR**7, u4 * u4)
    return jnp.where(value < 0, -power, power).astype(jnp.bfloat16)


def decode(code):
    y = code.astype(jnp.float32)
    a = jnp.abs(y)
    fourth = lax.rsqrt(lax.rsqrt(a))
    root = jnp.where(a < LINEAR**8, a * (LINEAR**-7 / GAIN), fourth * lax.rsqrt(fourth) * (1.0 / GAIN))
    return jnp.where(y < 0, -root, root)


def plain(grads, master, moment1, moment2, ema):
    local = grads[0]
    elements = local.shape[1] * local.shape[2] * lax.axis_size("tensor")
    summed = jnp.sum(local.astype(jnp.float32), axis=0)
    grad_part = lax.psum_scatter(summed, "shard", scatter_dimension=0, tiled=True)
    sq = lax.psum(jnp.sum(grad_part * grad_part), ("shard", "tensor"))
    scale = jnp.minimum(1.0, 1.0 / jnp.sqrt(sq / elements + 1e-06))
    clipped = scale * grad_part
    new_moment1 = beta_one * moment1 + (1.0 - beta_one) * clipped
    new_moment2 = beta_two * moment2 + (1.0 - beta_two) * clipped * clipped
    first_hat = new_moment1 / (1.0 - beta_one**STEP)
    second_hat = new_moment2 / (1.0 - beta_two**STEP)
    new_master = master - learn_rate * (
        first_hat / (jnp.sqrt(second_hat) + 1e-08) + decay_weight * master
    )
    new_ema = ema_keep * ema + (1.0 - ema_keep) * new_master
    weights = lax.all_gather(new_master.astype(jnp.bfloat16), "shard", axis=0, tiled=True)
    return (new_master, new_moment1, new_moment2, new_ema, weights)


def update(clipped, master, moment1, moment2):
    new_moment1 = beta_one * moment1 + (1.0 - beta_one) * clipped
    new_moment2 = beta_two * moment2 + (1.0 - beta_two) * clipped * clipped
    first_hat = new_moment1 / (1.0 - beta_one**STEP)
    second_hat = new_moment2 / (1.0 - beta_two**STEP)
    new_master = master - learn_rate * (
        first_hat / (jnp.sqrt(second_hat) + 1e-08) + decay_weight * master
    )
    return new_master, new_moment1, new_moment2


def make_kernel(n_tensor, micro, rows, cols):
    n_shard = 8
    devices = n_shard * n_tensor
    elements = n_shard * rows * cols * n_tensor
    piece = rows // PIECES

    def kernel(g, ma, m1, m2, o_clip, o_w,
               gv, st, part, sx, rx, sz, rz, w, sq_a,
               load_sem, store_sem, send_sem, recv_sem, sqs_sem, sqr_sem):
        s = lax.axis_index("shard")
        t = lax.axis_index("tensor")
        me = s * n_tensor + t
        x = lax.rem(s, 2)
        z = s // 2
        other = 1 - x
        zs = (z, z + 1 - 2 * lax.rem(z, 2), lax.rem(z + 2, 4), 3 - z)
        to_x = {"shard": 2 * z + other}
        to_z = {1: {"shard": 2 * zs[1] + x}, 2: {"shard": 2 * zs[2] + x}}

        def block(j, xx):
            return pl.ds(pl.multiple_of((2 * zs[j] + xx) * rows, rows), rows)

        loads = {}
        for i, (j, mine) in enumerate(((3, False), (2, False), (3, True), (1, False), (0, False),
                                       (2, True), (1, True), (0, True))):
            loads[j, mine] = (i, pltpu.make_async_copy(
                g.at[0, :, block(j, x if mine else other), :], gv.at[i], load_sem.at[i]))
            loads[j, mine][1].start()
        state = []
        for i, ref in enumerate((ma, m1, m2)):
            state.append(pltpu.make_async_copy(ref, st.at[i], load_sem.at[8 + i]))
            state[-1].start()

        def peer(k):
            index = lax.rem(me + k, devices)
            return {"shard": index // n_tensor, "tensor": lax.rem(index, n_tensor)}

        barrier = pltpu.get_barrier_semaphore()
        for k in range(1, devices):
            pl.semaphore_signal(barrier, inc=1, device_id=peer(k), device_id_type=MESH)

        def tiles(body, h, init=0):
            def step(i, carry):
                return body(pl.ds(pl.multiple_of(h * piece + i * TILE, TILE), TILE), carry)
            return lax.fori_loop(0, piece // TILE, step, init, unroll=True)

        def micro_sum(slot, r):
            total = gv[slot, 0, r, :].astype(jnp.float32)
            for m in range(1, micro):
                total = total + gv[slot, m, r, :].astype(jnp.float32)
            return total

        sent = []

        def send(src, dst, index, h, target):
            span = pl.ds(h * piece, piece)
            copy = pltpu.make_async_remote_copy(
                src_ref=src.at[span], dst_ref=dst.at[span],
                send_sem=send_sem.at[index, h], recv_sem=recv_sem.at[index, h],
                device_id=target, device_id_type=MESH)
            copy.start()
            sent.append(copy)
            return copy

        over_x = {}

        def give(j):
            slot, copy = loads[j, False]
            copy.wait()
            for h in range(PIECES):
                def body(r, c):
                    sx[j, r, :] = encode(micro_sum(slot, r))
                    return c
                tiles(body, h)
                if not over_x:
                    pl.semaphore_wait(barrier, devices - 1)
                over_x[j, h] = send(sx.at[j], rx.at[j], j, h, to_x)

        def keep(j):
            slot, copy = loads[j, True]
            copy.wait()

            def body(r, c):
                part[j, r, :] = micro_sum(slot, r)
                return c
            for h in range(PIECES):
                tiles(body, h)

        give(3)
        give(2)
        keep(3)
        give(1)
        give(0)
        keep(2)
        keep(1)
        keep(0)

        first, far, near = [], [], []
        for h in range(PIECES):
            over_x[3, h].wait_recv()

            def body(r, c):
                sz[0, r, :] = encode(part[3, r, :] + decode(rx[3, r, :]))
                return c
            tiles(body, h)
            first.append(send(sz.at[0], rz.at[0], 4, h, to_z[1]))
        for h in range(PIECES):
            over_x[2, h].wait_recv()
            first[h].wait_recv()

            def body(r, c):
                sz[1, r, :] = encode(part[2, r, :] + decode(rx[2, r, :]) + decode(rz[0, r, :]))
                return c
            tiles(body, h)
            far.append(send(sz.at[1], rz.at[1], 5, h, to_z[2]))
        for h in range(PIECES):
            over_x[1, h].wait_recv()

            def body(r, c):
                sz[2, r, :] = encode(part[1, r, :] + decode(rx[1, r, :]))
                return c
            tiles(body, h)
            near.append(send(sz.at[2], rz.at[2], 6, h, to_z[1]))

        acc = jnp.zeros((8, cols // 2), jnp.float32)
        for h in range(PIECES):
            over_x[0, h].wait_recv()
            near[h].wait_recv()
            far[h].wait_recv()

            def body(r, acc):
                total = part[0, r, :] + decode(rx[0, r, :]) + decode(rz[2, r, :]) + decode(rz[1, r, :])
                part[0, r, :] = total
                square = total * total
                square = square[:, :cols // 2] + square[:, cols // 2:]
                return acc + jnp.sum(square.reshape(TILE // 8, 8, cols // 2), axis=0)
            acc = tiles(body, h, acc)

        sq_a[me] = jnp.sum(acc, axis=0, keepdims=True)
        for k in range(1, devices):
            pltpu.make_async_remote_copy(
                src_ref=sq_a.at[me], dst_ref=sq_a.at[me], send_sem=sqs_sem, recv_sem=sqr_sem,
                device_id=peer(k), device_id_type=MESH).start()
        for copy in state:
            copy.wait()
        others = sq_a.at[pl.ds(0, devices - 1)]
        pltpu.make_async_copy(others, others, sqr_sem).wait()
        sq = jnp.sum(jnp.sum(sq_a[...], axis=0), axis=1, keepdims=True)
        scale = jnp.minimum(1.0, 1.0 / jnp.sqrt(sq / elements + 1e-06))

        def gathered(slot, index, h, target):
            return send(w.at[slot], w.at[slot], index, h, target)

        slot_x = [2 * zj + x for zj in zs]
        slot_o = [2 * zj + other for zj in zs]
        stores = []

        def store(src, dst):
            copy = pltpu.make_async_copy(src, dst, store_sem.at[len(stores)])
            copy.start()
            stores.append(copy)

        def store_w(slot, h):
            store(w.at[slot, pl.ds(h * piece, piece)],
                  o_w.at[pl.ds(pl.multiple_of(slot * rows + h * piece, piece), piece), :])

        far, near, side = [], [], []
        for h in range(PIECES):
            def body(r, c):
                clipped = scale * part[0, r, :]
                part[0, r, :] = clipped
                w[s, r, :] = update(clipped, st[0, r, :], st[1, r, :], st[2, r, :])[0].astype(jnp.bfloat16)
                return c
            tiles(body, h)
            far.append(gathered(s, 9, h, to_z[2]))
            near.append(gathered(s, 8, h, to_z[1]))
            side.append(gathered(s, 7, h, to_x))
            store_w(s, h)
        store(part.at[0], o_clip)

        near_2, ends = [], []
        for h in range(PIECES):
            near[h].wait_recv()
            ends.append((gathered(slot_x[1], 11, h, to_x), 1, h))
            store_w(slot_x[1], h)
            far[h].wait_recv()
            near_2.append(gathered(slot_x[2], 10, h, to_z[1]))
            ends.append((gathered(slot_x[2], 12, h, to_x), 2, h))
            store_w(slot_x[2], h)
        for h in range(PIECES):
            side[h].wait_recv()
            store_w(slot_o[0], h)
        for h in range(PIECES):
            near_2[h].wait_recv()
            ends.append((gathered(slot_x[3], 13, h, to_x), 3, h))
            store_w(slot_x[3], h)
        for copy, j, h in ends:
            copy.wait_recv()
            store_w(slot_o[j], h)
        for copy in sent:
            copy.wait_send()
        pltpu.make_async_copy(others, others, sqs_sem).wait()
        for copy in stores:
            copy.wait()

    return kernel


def fused(grads, master, moment1, moment2, ema):
    n_tensor = lax.axis_size("tensor")
    micro = grads.shape[1]
    rows, cols = master.shape
    f32 = jax.ShapeDtypeStruct((rows, cols), jnp.float32)
    full = jax.ShapeDtypeStruct((8 * rows, cols), jnp.bfloat16)
    anywhere = pl.BlockSpec(memory_space=pl.ANY)
    clipped, weights = pl.pallas_call(
        make_kernel(n_tensor, micro, rows, cols),
        out_shape=(f32, full),
        in_specs=[anywhere] * 4,
        out_specs=(anywhere,) * 2,
        scratch_shapes=[
            pltpu.VMEM((8, micro, rows, cols), jnp.bfloat16),
            pltpu.VMEM((3, rows, cols), jnp.float32),
            pltpu.VMEM((4, rows, cols), jnp.float32),
            pltpu.VMEM((4, rows, cols), jnp.bfloat16),
            pltpu.VMEM((4, rows, cols), jnp.bfloat16),
            pltpu.VMEM((3, rows, cols), jnp.bfloat16),
            pltpu.VMEM((3, rows, cols), jnp.bfloat16),
            pltpu.VMEM((8, rows, cols), jnp.bfloat16),
            pltpu.VMEM((8 * n_tensor, 1, cols // 2), jnp.float32),
            pltpu.SemaphoreType.DMA((11,)),
            pltpu.SemaphoreType.DMA((8 * PIECES + 1,)),
            pltpu.SemaphoreType.DMA((14, PIECES)),
            pltpu.SemaphoreType.DMA((14, PIECES)),
            pltpu.SemaphoreType.DMA,
            pltpu.SemaphoreType.DMA,
        ],
        compiler_params=pltpu.CompilerParams(
            collective_id=0, has_side_effects=True, vmem_limit_bytes=64 * 1024 * 1024
        ),
        cost_estimate=pl.CostEstimate(flops=20_000_000, bytes_accessed=6_000_000, transcendentals=300_000),
    )(grads, master, moment1, moment2)
    new_master, new_moment1, new_moment2 = update(clipped, master, moment1, moment2)
    new_ema = ema_keep * ema + (1.0 - ema_keep) * new_master
    return (new_master, new_moment1, new_moment2, new_ema, weights)


def solution(mesh):
    def shards(grads, master, moment1, moment2, ema):
        if mesh.shape["shard"] == 8 and master.shape[0] % (PIECES * TILE) == 0 and master.shape[1] == 256:
            return fused(grads, master, moment1, moment2, ema)
        return plain(grads, master, moment1, moment2, ema)

    return jax.shard_map(
        shards,
        mesh=mesh,
        in_specs=(
            P("shard", None, None, "tensor"),
            P("shard", "tensor"),
            P("shard", "tensor"),
            P("shard", "tensor"),
            P("shard", "tensor"),
        ),
        out_specs=(
            P("shard", "tensor"),
            P("shard", "tensor"),
            P("shard", "tensor"),
            P("shard", "tensor"),
            P(None, "tensor"),
        ),
        check_vma=False,
    )
```

```python
import jax
import jax.numpy as jnp
from jax import lax
from jax.experimental import pallas as pl
from jax.experimental.pallas import tpu as pltpu
from jax.sharding import PartitionSpec as P

STEP = 10

beta_one = 0.9
beta_two = 0.95
learn_rate = 0.02
decay_weight = 0.1
ema_keep = 0.99

MESH = pl.DeviceIdType.MESH
TILE = 32
PIECES = 2
LAST = PIECES - 1

GAIN = 16.0
LINEAR = 2.0**-12


def encode(value):
    u = jnp.abs(value) * GAIN
    u2 = u * u
    u4 = u2 * u2
    power = jnp.where(u < LINEAR, u * LINEAR**7, u4 * u4)
    return jnp.where(value < 0, -power, power).astype(jnp.bfloat16)


def decode(code):
    y = code.astype(jnp.float32)
    a = jnp.abs(y)
    fourth = lax.rsqrt(lax.rsqrt(a))
    root = jnp.where(a < LINEAR**8, a * (LINEAR**-7 / GAIN), fourth * lax.rsqrt(fourth) * (1.0 / GAIN))
    return jnp.where(y < 0, -root, root)


def plain(grads, master, moment1, moment2, ema):
    local = grads[0]
    elements = local.shape[1] * local.shape[2] * lax.axis_size("tensor")
    summed = jnp.sum(local.astype(jnp.float32), axis=0)
    grad_part = lax.psum_scatter(summed, "shard", scatter_dimension=0, tiled=True)
    sq = lax.psum(jnp.sum(grad_part * grad_part), ("shard", "tensor"))
    scale = jnp.minimum(1.0, 1.0 / jnp.sqrt(sq / elements + 1e-06))
    clipped = scale * grad_part
    new_moment1 = beta_one * moment1 + (1.0 - beta_one) * clipped
    new_moment2 = beta_two * moment2 + (1.0 - beta_two) * clipped * clipped
    first_hat = new_moment1 / (1.0 - beta_one**STEP)
    second_hat = new_moment2 / (1.0 - beta_two**STEP)
    new_master = master - learn_rate * (
        first_hat / (jnp.sqrt(second_hat) + 1e-08) + decay_weight * master
    )
    new_ema = ema_keep * ema + (1.0 - ema_keep) * new_master
    weights = lax.all_gather(new_master.astype(jnp.bfloat16), "shard", axis=0, tiled=True)
    return (new_master, new_moment1, new_moment2, new_ema, weights)


def update(clipped, master, moment1, moment2):
    new_moment1 = beta_one * moment1 + (1.0 - beta_one) * clipped
    new_moment2 = beta_two * moment2 + (1.0 - beta_two) * clipped * clipped
    first_hat = new_moment1 / (1.0 - beta_one**STEP)
    second_hat = new_moment2 / (1.0 - beta_two**STEP)
    new_master = master - learn_rate * (
        first_hat / (jnp.sqrt(second_hat) + 1e-08) + decay_weight * master
    )
    return new_master, new_moment1, new_moment2


def make_kernel(n_tensor, micro, rows, cols):
    n_shard = 8
    devices = n_shard * n_tensor
    elements = n_shard * rows * cols * n_tensor
    piece = rows // PIECES

    def kernel(g, ma, m1, m2, o_clip, w,
               gv, st, part, sx, rx, sz, rz, sq_a,
               load_sem, send_sem, recv_sem, sqs_sem, sqr_sem):
        s = lax.axis_index("shard")
        t = lax.axis_index("tensor")
        me = s * n_tensor + t
        x = lax.rem(s, 2)
        z = s // 2
        other = 1 - x
        zs = (z, z + 1 - 2 * lax.rem(z, 2), lax.rem(z + 2, 4), 3 - z)
        to_x = {"shard": 2 * z + other}
        to_z = {1: {"shard": 2 * zs[1] + x}, 2: {"shard": 2 * zs[2] + x}}

        def block(j, xx):
            return pl.ds(pl.multiple_of((2 * zs[j] + xx) * rows, rows), rows)

        loads = {}
        for i, (j, mine) in enumerate(((3, False), (1, False), (2, False), (3, True), (0, False),
                                       (2, True), (1, True), (0, True))):
            loads[j, mine] = (i, pltpu.make_async_copy(
                g.at[0, :, block(j, x if mine else other), :], gv.at[i], load_sem.at[i]))
            loads[j, mine][1].start()
        state = []
        for i, ref in enumerate((ma, m1, m2)):
            state.append(pltpu.make_async_copy(ref, st.at[i], load_sem.at[8 + i]))
            state[-1].start()

        def peer(k):
            index = lax.rem(me + k, devices)
            return {"shard": index // n_tensor, "tensor": lax.rem(index, n_tensor)}

        barrier = pltpu.get_barrier_semaphore()
        for k in range(1, devices):
            pl.semaphore_signal(barrier, inc=1, device_id=peer(k), device_id_type=MESH)

        def tiles(body, h, init=0):
            def step(i, carry):
                return body(pl.ds(pl.multiple_of(h * piece + i * TILE, TILE), TILE), carry)
            return lax.fori_loop(0, piece // TILE, step, init, unroll=True)

        def micro_sum(slot, r):
            total = gv[slot, 0, r, :].astype(jnp.float32)
            for m in range(1, micro):
                total = total + gv[slot, m, r, :].astype(jnp.float32)
            return total

        sent = []

        def send(src, dst, index, h, target):
            span = pl.ds(h * piece, piece)
            copy = pltpu.make_async_remote_copy(
                src_ref=src.at[span], dst_ref=dst.at[span],
                send_sem=send_sem.at[index, h], recv_sem=recv_sem.at[index, h],
                device_id=target, device_id_type=MESH)
            copy.start()
            sent.append(copy)
            return copy

        over_x = {}

        def give(j, pieces=range(PIECES)):
            slot, copy = loads[j, False]
            if j != 1 or LAST in pieces:
                copy.wait()
            for h in pieces:
                if (j, h) == (0, LAST):
                    over_x[1, LAST].wait_recv()

                def body(r, c):
                    total = micro_sum(slot, r)
                    if (j, h) == (0, LAST):
                        total = total + decode(rz[3, r, :])
                    sx[j, r, :] = encode(total)
                    return c
                tiles(body, h)
                if not over_x:
                    pl.semaphore_wait(barrier, devices - 1)
                if (j, h) == (1, LAST):
                    over_x[j, h] = send(sx.at[j], rz.at[3], 14, h, to_z[1])
                else:
                    over_x[j, h] = send(sx.at[j], rx.at[j], j, h, to_x)

        def keep(j):
            slot, copy = loads[j, True]
            copy.wait()

            def body(r, c):
                part[j, r, :] = micro_sum(slot, r)
                return c
            for h in range(PIECES):
                tiles(body, h)

        give(3)
        give(1, (LAST,))
        give(2)
        keep(3)
        give(1, range(LAST))
        keep(2)
        keep(1)
        keep(0)
        give(0)

        first, far, near = [], [], []
        for h in range(PIECES):
            over_x[3, h].wait_recv()

            def body(r, c):
                sz[0, r, :] = encode(part[3, r, :] + decode(rx[3, r, :]))
                return c
            tiles(body, h)
            first.append(send(sz.at[0], rz.at[0], 4, h, to_z[1]))
        for h in range(PIECES):
            over_x[2, h].wait_recv()
            first[h].wait_recv()

            def body(r, c):
                sz[1, r, :] = encode(part[2, r, :] + decode(rx[2, r, :]) + decode(rz[0, r, :]))
                return c
            tiles(body, h)
            far.append(send(sz.at[1], rz.at[1], 5, h, to_z[2]))
        for h in range(PIECES):
            if h != LAST:
                over_x[1, h].wait_recv()

            def body(r, c):
                total = part[1, r, :]
                if h != LAST:
                    total = total + decode(rx[1, r, :])
                sz[2, r, :] = encode(total)
                return c
            tiles(body, h)
            near.append(send(sz.at[2], rz.at[2], 6, h, to_z[1]))

        acc = jnp.zeros((8, cols // 2), jnp.float32)
        for h in range(PIECES):
            over_x[0, h].wait_recv()
            near[h].wait_recv()
            far[h].wait_recv()

            def body(r, acc):
                total = part[0, r, :] + decode(rx[0, r, :]) + decode(rz[2, r, :]) + decode(rz[1, r, :])
                part[0, r, :] = total
                square = total * total
                square = square[:, :cols // 2] + square[:, cols // 2:]
                return acc + jnp.sum(square.reshape(TILE // 8, 8, cols // 2), axis=0)
            acc = tiles(body, h, acc)

        sq_a[me] = jnp.sum(acc, axis=0, keepdims=True)
        for k in range(1, devices):
            pltpu.make_async_remote_copy(
                src_ref=sq_a.at[me], dst_ref=sq_a.at[me], send_sem=sqs_sem, recv_sem=sqr_sem,
                device_id=peer(k), device_id_type=MESH).start()
        for copy in state:
            copy.wait()
        others = sq_a.at[pl.ds(0, devices - 1)]
        pltpu.make_async_copy(others, others, sqr_sem).wait()
        sq = jnp.sum(jnp.sum(sq_a[...], axis=0), axis=1, keepdims=True)
        scale = jnp.minimum(1.0, 1.0 / jnp.sqrt(sq / elements + 1e-06))

        def gathered(slot, index, h, target):
            return send(w.at[slot], w.at[slot], index, h, target)

        slot_x = [2 * zj + x for zj in zs]
        slot_o = [2 * zj + other for zj in zs]
        far, near, side = [], [], []
        for h in range(PIECES):
            def body(r, c):
                clipped = scale * part[0, r, :]
                o_clip[r, :] = clipped
                w[s, r, :] = update(clipped, st[0, r, :], st[1, r, :], st[2, r, :])[0].astype(jnp.bfloat16)
                return c
            tiles(body, h)
            far.append(gathered(s, 9, h, to_z[2]))
            near.append(gathered(s, 8, h, to_z[1]))
            side.append(gathered(s, 7, h, to_x))

        near_2, ends = [], []
        for h in range(PIECES):
            near[h].wait_recv()
            if h != LAST:
                ends.append((gathered(slot_x[1], 11, h, to_x), 1, h))
            far[h].wait_recv()
            near_2.append(gathered(slot_x[2], 10, h, to_z[1]))
            ends.append((gathered(slot_x[2], 12, h, to_x), 2, h))
            if h == 0:
                side[LAST].wait_recv()
                ends.append((gathered(slot_o[0], 11, LAST, to_z[1]), 1, LAST))
        for h in range(LAST):
            side[h].wait_recv()
        for h in range(PIECES):
            near_2[h].wait_recv()
            ends.append((gathered(slot_x[3], 13, h, to_x), 3, h))
        for copy, j, h in ends:
            copy.wait_recv()
        for copy in sent:
            copy.wait_send()
        pltpu.make_async_copy(others, others, sqs_sem).wait()

    return kernel


def fused(grads, master, moment1, moment2, ema):
    n_tensor = lax.axis_size("tensor")
    micro = grads.shape[1]
    rows, cols = master.shape
    f32 = jax.ShapeDtypeStruct((rows, cols), jnp.float32)
    full = jax.ShapeDtypeStruct((8, rows, cols), jnp.bfloat16)
    anywhere = pl.BlockSpec(memory_space=pl.ANY)
    clipped, weights = pl.pallas_call(
        make_kernel(n_tensor, micro, rows, cols),
        out_shape=(pltpu.VMEM(f32.shape, f32.dtype), pltpu.VMEM(full.shape, full.dtype)),
        in_specs=[anywhere] * 4,
        out_specs=(pl.BlockSpec(memory_space=pltpu.VMEM),) * 2,
        scratch_shapes=[
            pltpu.VMEM((8, micro, rows, cols), jnp.bfloat16),
            pltpu.VMEM((3, rows, cols), jnp.float32),
            pltpu.VMEM((4, rows, cols), jnp.float32),
            pltpu.VMEM((4, rows, cols), jnp.bfloat16),
            pltpu.VMEM((4, rows, cols), jnp.bfloat16),
            pltpu.VMEM((3, rows, cols), jnp.bfloat16),
            pltpu.VMEM((4, rows, cols), jnp.bfloat16),
            pltpu.VMEM((8 * n_tensor, 1, cols // 2), jnp.float32),
            pltpu.SemaphoreType.DMA((11,)),
            pltpu.SemaphoreType.DMA((15, PIECES)),
            pltpu.SemaphoreType.DMA((15, PIECES)),
            pltpu.SemaphoreType.DMA,
            pltpu.SemaphoreType.DMA,
        ],
        compiler_params=pltpu.CompilerParams(
            collective_id=0, has_side_effects=True, vmem_limit_bytes=63 * 1024 * 1024
        ),
        cost_estimate=pl.CostEstimate(flops=20_000_000, bytes_accessed=6_000_000, transcendentals=300_000),
    )(grads, master, moment1, moment2)
    new_master, new_moment1, new_moment2 = update(clipped, master, moment1, moment2)
    new_ema = ema_keep * ema + (1.0 - ema_keep) * new_master
    return (new_master, new_moment1, new_moment2, new_ema, weights.reshape(8 * rows, cols))


def solution(mesh):
    def shards(grads, master, moment1, moment2, ema):
        if mesh.shape["shard"] == 8 and master.shape[0] % (PIECES * TILE) == 0 and master.shape[1] == 256:
            return fused(grads, master, moment1, moment2, ema)
        return plain(grads, master, moment1, moment2, ema)

    return jax.shard_map(
        shards,
        mesh=mesh,
        in_specs=(
            P("shard", None, None, "tensor"),
            P("shard", "tensor"),
            P("shard", "tensor"),
            P("shard", "tensor"),
            P("shard", "tensor"),
        ),
        out_specs=(
            P("shard", "tensor"),
            P("shard", "tensor"),
            P("shard", "tensor"),
            P("shard", "tensor"),
            P(None, "tensor"),
        ),
        check_vma=False,
    )
```

```python
import jax
import jax.numpy as jnp
from jax import lax
from jax.experimental import pallas as pl
from jax.experimental.pallas import tpu as pltpu
from jax.sharding import PartitionSpec as P

STEP = 10

beta_one = 0.9
beta_two = 0.95
learn_rate = 0.02
decay_weight = 0.1
ema_keep = 0.99

MESH = pl.DeviceIdType.MESH
TILE = 32
PIECES = 3
LAST = PIECES - 1

GAIN = 16.0
LINEAR = 2.0**-12


def encode(value):
    u = jnp.abs(value) * GAIN
    u2 = u * u
    u4 = u2 * u2
    power = jnp.where(u < LINEAR, u * LINEAR**7, u4 * u4)
    return jnp.where(value < 0, -power, power).astype(jnp.bfloat16)


def decode(code):
    y = code.astype(jnp.float32)
    a = jnp.abs(y)
    fourth = lax.rsqrt(lax.rsqrt(a))
    root = jnp.where(a < LINEAR**8, a * (LINEAR**-7 / GAIN), fourth * lax.rsqrt(fourth) * (1.0 / GAIN))
    return jnp.where(y < 0, -root, root)


def plain(grads, master, moment1, moment2, ema):
    local = grads[0]
    elements = local.shape[1] * local.shape[2] * lax.axis_size("tensor")
    summed = jnp.sum(local.astype(jnp.float32), axis=0)
    grad_part = lax.psum_scatter(summed, "shard", scatter_dimension=0, tiled=True)
    sq = lax.psum(jnp.sum(grad_part * grad_part), ("shard", "tensor"))
    scale = jnp.minimum(1.0, 1.0 / jnp.sqrt(sq / elements + 1e-06))
    clipped = scale * grad_part
    new_moment1 = beta_one * moment1 + (1.0 - beta_one) * clipped
    new_moment2 = beta_two * moment2 + (1.0 - beta_two) * clipped * clipped
    first_hat = new_moment1 / (1.0 - beta_one**STEP)
    second_hat = new_moment2 / (1.0 - beta_two**STEP)
    new_master = master - learn_rate * (
        first_hat / (jnp.sqrt(second_hat) + 1e-08) + decay_weight * master
    )
    new_ema = ema_keep * ema + (1.0 - ema_keep) * new_master
    weights = lax.all_gather(new_master.astype(jnp.bfloat16), "shard", axis=0, tiled=True)
    return (new_master, new_moment1, new_moment2, new_ema, weights)


def update(clipped, master, moment1, moment2):
    new_moment1 = beta_one * moment1 + (1.0 - beta_one) * clipped
    new_moment2 = beta_two * moment2 + (1.0 - beta_two) * clipped * clipped
    first_hat = new_moment1 / (1.0 - beta_one**STEP)
    second_hat = new_moment2 / (1.0 - beta_two**STEP)
    new_master = master - learn_rate * (
        first_hat / (jnp.sqrt(second_hat) + 1e-08) + decay_weight * master
    )
    return new_master, new_moment1, new_moment2


def make_kernel(n_tensor, micro, rows, cols):
    n_shard = 8
    devices = n_shard * n_tensor
    elements = n_shard * rows * cols * n_tensor
    piece = rows // PIECES

    def kernel(g, ma, m1, m2, em, o_ma, o_m1, o_m2, o_em, w,
               gv, st, part, sx, rx, sz, rz, sq_a,
               load_sem, send_sem, recv_sem, sqs_sem, sqr_sem):
        s = lax.axis_index("shard")
        t = lax.axis_index("tensor")
        me = s * n_tensor + t
        x = lax.rem(s, 2)
        z = s // 2
        other = 1 - x
        zs = (z, z + 1 - 2 * lax.rem(z, 2), lax.rem(z + 2, 4), 3 - z)
        to_x = {"shard": 2 * z + other}
        to_z = {1: {"shard": 2 * zs[1] + x}, 2: {"shard": 2 * zs[2] + x}}

        def block(j, xx):
            return pl.ds(pl.multiple_of((2 * zs[j] + xx) * rows, rows), rows)

        loads = {}
        for i, (j, mine) in enumerate(((3, False), (1, False), (2, False), (3, True), (0, False),
                                       (2, True), (1, True), (0, True))):
            loads[j, mine] = (i, pltpu.make_async_copy(
                g.at[0, :, block(j, x if mine else other), :], gv.at[i], load_sem.at[i]))
            loads[j, mine][1].start()
        state = []
        for i, ref in enumerate((ma, m1, m2, em)):
            state.append(pltpu.make_async_copy(ref, st.at[i], load_sem.at[8 + i]))
            state[-1].start()

        def peer(k):
            index = lax.rem(me + k, devices)
            return {"shard": index // n_tensor, "tensor": lax.rem(index, n_tensor)}

        barrier = pltpu.get_barrier_semaphore()
        for k in range(1, devices):
            pl.semaphore_signal(barrier, inc=1, device_id=peer(k), device_id_type=MESH)

        def tiles(body, h, init=0):
            def step(i, carry):
                return body(pl.ds(pl.multiple_of(h * piece + i * TILE, TILE), TILE), carry)
            return lax.fori_loop(0, piece // TILE, step, init, unroll=True)

        def micro_sum(slot, r):
            total = gv[slot, 0, r, :].astype(jnp.float32)
            for m in range(1, micro):
                total = total + gv[slot, m, r, :].astype(jnp.float32)
            return total

        sent = []

        def send(src, dst, index, h, target):
            span = pl.ds(h * piece, piece)
            copy = pltpu.make_async_remote_copy(
                src_ref=src.at[span], dst_ref=dst.at[span],
                send_sem=send_sem.at[index, h], recv_sem=recv_sem.at[index, h],
                device_id=target, device_id_type=MESH)
            copy.start()
            sent.append(copy)
            return copy

        over_x = {}

        def give(j, pieces=range(PIECES)):
            slot, copy = loads[j, False]
            if j != 1 or LAST in pieces:
                copy.wait()
            for h in pieces:
                if (j, h) == (0, LAST):
                    over_x[1, LAST].wait_recv()

                def body(r, c):
                    total = micro_sum(slot, r)
                    if (j, h) == (0, LAST):
                        total = total + decode(rz[3, r, :])
                    sx[j, r, :] = encode(total)
                    return c
                tiles(body, h)
                if not over_x:
                    pl.semaphore_wait(barrier, devices - 1)
                if (j, h) == (1, LAST):
                    over_x[j, h] = send(sx.at[j], rz.at[3], 14, h, to_z[1])
                else:
                    over_x[j, h] = send(sx.at[j], rx.at[j], j, h, to_x)

        def keep(j):
            slot, copy = loads[j, True]
            copy.wait()

            def body(r, c):
                part[j, r, :] = micro_sum(slot, r)
                return c
            for h in range(PIECES):
                tiles(body, h)

        give(3)
        give(1, (LAST,))
        give(2)
        keep(3)
        give(1, range(LAST))
        keep(2)
        keep(1)
        keep(0)
        give(0)

        first, far, near = [], [], []
        for h in range(PIECES):
            over_x[3, h].wait_recv()

            def body(r, c):
                sz[0, r, :] = encode(part[3, r, :] + decode(rx[3, r, :]))
                return c
            tiles(body, h)
            first.append(send(sz.at[0], rz.at[0], 4, h, to_z[1]))
        for h in range(PIECES):
            over_x[2, h].wait_recv()
            first[h].wait_recv()

            def body(r, c):
                sz[1, r, :] = encode(part[2, r, :] + decode(rx[2, r, :]) + decode(rz[0, r, :]))
                return c
            tiles(body, h)
            far.append(send(sz.at[1], rz.at[1], 5, h, to_z[2]))
        for h in range(PIECES):
            if h != LAST:
                over_x[1, h].wait_recv()

            def body(r, c):
                total = part[1, r, :]
                if h != LAST:
                    total = total + decode(rx[1, r, :])
                sz[2, r, :] = encode(total)
                return c
            tiles(body, h)
            near.append(send(sz.at[2], rz.at[2], 6, h, to_z[1]))

        acc = jnp.zeros((8, cols // 2), jnp.float32)
        for h in range(PIECES):
            over_x[0, h].wait_recv()
            near[h].wait_recv()
            far[h].wait_recv()

            def body(r, acc):
                total = part[0, r, :] + decode(rx[0, r, :]) + decode(rz[2, r, :]) + decode(rz[1, r, :])
                part[0, r, :] = total
                square = total * total
                square = square[:, :cols // 2] + square[:, cols // 2:]
                return acc + jnp.sum(square.reshape(TILE // 8, 8, cols // 2), axis=0)
            acc = tiles(body, h, acc)

        sq_a[me] = jnp.sum(acc, axis=0, keepdims=True)
        for k in range(1, devices):
            pltpu.make_async_remote_copy(
                src_ref=sq_a.at[me], dst_ref=sq_a.at[me], send_sem=sqs_sem, recv_sem=sqr_sem,
                device_id=peer(k), device_id_type=MESH).start()
        for copy in state:
            copy.wait()
        others = sq_a.at[pl.ds(0, devices - 1)]
        pltpu.make_async_copy(others, others, sqr_sem).wait()
        sq = jnp.sum(jnp.sum(sq_a[...], axis=0), axis=1, keepdims=True)
        scale = jnp.minimum(1.0, 1.0 / jnp.sqrt(sq / elements + 1e-06))

        def gathered(slot, index, h, target):
            return send(w.at[slot], w.at[slot], index, h, target)

        slot_x = [2 * zj + x for zj in zs]
        slot_o = [2 * zj + other for zj in zs]
        far, near, side = [], [], []
        for h in range(PIECES):
            def body(r, c):
                clipped = scale * part[0, r, :]
                new_ma, new_m1, new_m2 = update(clipped, st[0, r, :], st[1, r, :], st[2, r, :])
                w[s, r, :] = new_ma.astype(jnp.bfloat16)
                o_ma[r, :] = new_ma
                o_m1[r, :] = new_m1
                o_m2[r, :] = new_m2
                return c
            tiles(body, h)
            far.append(gathered(s, 9, h, to_z[2]))
            near.append(gathered(s, 8, h, to_z[1]))
            side.append(gathered(s, 7, h, to_x))

        def body(r, c):
            o_em[r, :] = ema_keep * st[3, r, :] + (1.0 - ema_keep) * o_ma[r, :]
            return c
        for h in range(PIECES):
            tiles(body, h)

        near_2, ends = [], []
        for h in range(PIECES):
            near[h].wait_recv()
            if h != LAST:
                ends.append((gathered(slot_x[1], 11, h, to_x), 1, h))
            far[h].wait_recv()
            near_2.append(gathered(slot_x[2], 10, h, to_z[1]))
            ends.append((gathered(slot_x[2], 12, h, to_x), 2, h))
            if h == 0:
                side[LAST].wait_recv()
                ends.append((gathered(slot_o[0], 11, LAST, to_z[1]), 1, LAST))
        for h in range(LAST):
            side[h].wait_recv()
        for h in range(PIECES):
            near_2[h].wait_recv()
            ends.append((gathered(slot_x[3], 13, h, to_x), 3, h))
        for copy, j, h in ends:
            copy.wait_recv()
        for copy in sent:
            copy.wait_send()
        pltpu.make_async_copy(others, others, sqs_sem).wait()

    return kernel


def hand_over(*refs):
    copies = [pltpu.make_async_copy(refs[i], refs[5 + i], refs[10].at[i]) for i in range(5)]
    for copy in copies:
        copy.start()
    for copy in copies:
        copy.wait()


def fused(grads, master, moment1, moment2, ema):
    n_tensor = lax.axis_size("tensor")
    micro = grads.shape[1]
    rows, cols = master.shape
    f32 = jax.ShapeDtypeStruct((rows, cols), jnp.float32)
    full = jax.ShapeDtypeStruct((8, rows, cols), jnp.bfloat16)
    anywhere = pl.BlockSpec(memory_space=pl.ANY)
    inside = pl.BlockSpec(memory_space=pltpu.VMEM)
    results = pl.pallas_call(
        make_kernel(n_tensor, micro, rows, cols),
        out_shape=(pltpu.VMEM(f32.shape, f32.dtype),) * 4 + (pltpu.VMEM(full.shape, full.dtype),),
        in_specs=[anywhere] * 5,
        out_specs=(inside,) * 5,
        scratch_shapes=[
            pltpu.VMEM((8, micro, rows, cols), jnp.bfloat16),
            pltpu.VMEM((4, rows, cols), jnp.float32),
            pltpu.VMEM((4, rows, cols), jnp.float32),
            pltpu.VMEM((4, rows, cols), jnp.bfloat16),
            pltpu.VMEM((4, rows, cols), jnp.bfloat16),
            pltpu.VMEM((3, rows, cols), jnp.bfloat16),
            pltpu.VMEM((4, rows, cols), jnp.bfloat16),
            pltpu.VMEM((8 * n_tensor, 1, cols // 2), jnp.float32),
            pltpu.SemaphoreType.DMA((12,)),
            pltpu.SemaphoreType.DMA((15, PIECES)),
            pltpu.SemaphoreType.DMA((15, PIECES)),
            pltpu.SemaphoreType.DMA,
            pltpu.SemaphoreType.DMA,
        ],
        compiler_params=pltpu.CompilerParams(
            collective_id=0, has_side_effects=True, vmem_limit_bytes=63936 * 1024
        ),
        cost_estimate=pl.CostEstimate(flops=20_000_000, bytes_accessed=6_000_000, transcendentals=300_000),
    )(grads, master, moment1, moment2, ema)
    outputs = pl.pallas_call(
        hand_over,
        out_shape=(f32, f32, f32, f32, full),
        in_specs=[inside] * 5,
        out_specs=(anywhere,) * 5,
        scratch_shapes=[pltpu.SemaphoreType.DMA((5,))],
        compiler_params=pltpu.CompilerParams(vmem_limit_bytes=4 * 1024 * 1024),
        cost_estimate=pl.CostEstimate(flops=0, bytes_accessed=3_000_000, transcendentals=0),
    )(*results)
    return tuple(outputs[:4]) + (outputs[4].reshape(8 * rows, cols),)


def solution(mesh):
    def shards(grads, master, moment1, moment2, ema):
        if mesh.shape["shard"] == 8 and master.shape[0] % (PIECES * TILE) == 0 and master.shape[1] == 256:
            return fused(grads, master, moment1, moment2, ema)
        return plain(grads, master, moment1, moment2, ema)

    return jax.shard_map(
        shards,
        mesh=mesh,
        in_specs=(
            P("shard", None, None, "tensor"),
            P("shard", "tensor"),
            P("shard", "tensor"),
            P("shard", "tensor"),
            P("shard", "tensor"),
        ),
        out_specs=(
            P("shard", "tensor"),
            P("shard", "tensor"),
            P("shard", "tensor"),
            P("shard", "tensor"),
            P(None, "tensor"),
        ),
        check_vma=False,
    )
```
